32 devices in a mesh: grp: 2 (over y), seq: 4 (over z), chan: 4 (over x, core).
Axes of the slice: x: 2, y: 2, z: 4, core: 2. Of those that a mesh axis runs over, the one named last changes fastest.
Arguments:
- features: bfloat16 [1024, 3, 8192], P(('grp', 'seq'), None, 'chan'), parts along dimension 0, may hold values from -6 to 6
- conv_weight: bfloat16 [7, 3, 8192], P(None, None, 'chan'), may hold values from -2 to 2
- history: bfloat16 [12, 3, 8192], P('grp', None, 'chan'), parts along dimension 0, may hold values from -6 to 6
- pole_rate: float32 [16, 8192], P(None, 'chan'), may hold values from 0.00048828125 to 0.05
- residue: float32 [16, 8192], P(None, 'chan'), may hold values from -6 to 6
- skip_gain: float32 [8192], P('chan'), may hold values from -6 to 6
- start_state: float32 [32, 8192], P('grp', 'chan'), parts along dimension 0, may hold values from -96 to 96
Outputs:
- mixer_out: bfloat16 [1024, 8192], P(('grp', 'seq'), 'chan'), parts along dimension 0
The draws below stay inside these ranges and needn't reach their ends.
There are 2 independent parts, one for each index of `grp`. The reference program is written for one: setup_inputs(seed, part) draws one part's arguments, and reference() takes and returns one part's arrays. A program takes and returns all parts, laid end to end along the dimension named above; an argument that names none is the same for every part. Nothing has to cross between parts.
All inputs are finite; a program needn't handle non-finite values.
Results may differ from the reference program's by a relative error of at most 0.001.
Values may be sent and summed in bfloat16 or wider, within the bound.
A program may use at most 192 MiB of HBM per device.

```python
import math
import jax
import jax.numpy as jnp
from jax import lax

D = 8192
POLES = 16
KERNEL = 7
TOKENS = 512


def levels(rng, shape, pieces, least, largest):
    loudness = 1.0
    for position, shards_of in pieces:
        steps = jax.random.uniform(jax.random.fold_in(jax.random.fold_in(rng, 6), position), (shards_of,), jnp.float32, least / len(pieces), largest / len(pieces))
        loudness = loudness * jnp.repeat(jnp.exp(steps), shape[position] // shards_of).reshape((-1,) + (1,) * (len(shape) - 1 - position))
    return loudness


def gaussian(own_key, dims, deviation, reach, split=(), kind=jnp.bfloat16):
    result = deviation * jax.random.normal(own_key, dims, jnp.float32)
    if split:
        result = result * levels(own_key, dims, split, -0.22, 0.18)
    return jnp.clip(result, -reach, reach).astype(kind)


def setup_inputs(seed: int = 0, part: int = 0) -> dict:
    arg_keys = jax.random.split(jax.random.key(seed), 8)
    part_splits = jax.random.split(jax.random.fold_in(arg_keys[7], part), 8)
    features = gaussian(part_splits[0], (TOKENS, 3, D), 1.0, 6.0, ((0, 4), (2, 4)))
    conv_weight = gaussian(arg_keys[1], (KERNEL, 3, D), KERNEL ** -0.5, 2.0, ((2, 4),))
    history = gaussian(part_splits[2], (KERNEL - 1, 3, D), 1.0, 6.0, ((2, 4),))
    pole_rate = jnp.clip(jnp.exp(math.log(0.05) - 4.6288867 * jax.random.uniform(arg_keys[3], (POLES, D), jnp.float32) ** levels(arg_keys[3], (POLES, D), ((1, 4),), -0.2, 0.2)), 0.00048828125, 0.05)
    residue = gaussian(arg_keys[4], (POLES, D), 1.0, 6.0, ((1, 4),), jnp.float32)
    skip_gain = gaussian(arg_keys[5], (D,), 1.0, 6.0, ((0, 4),), jnp.float32)
    start_state = gaussian(part_splits[6], (POLES, D), 16.0, 96.0, ((1, 4),), jnp.float32)
    return dict(features=features, conv_weight=conv_weight, history=history, pole_rate=pole_rate, residue=residue, skip_gain=skip_gain, start_state=start_state)


def reference(features, conv_weight, history, pole_rate, residue, skip_gain, start_state):
    length = features.shape[0]
    margin = KERNEL - 1
    extended = jnp.concatenate([history, features], axis=0).astype(jnp.float32)
    taps = conv_weight.astype(jnp.float32)
    filtered = jnp.zeros(features.shape, jnp.float32)
    for i in range(KERNEL):
        filtered = filtered + taps[i] * extended[margin - i:margin - i + length]
    query_part = filtered[:, 0, :]
    product = filtered[:, 1, :] * filtered[:, 2, :]
    pole_decay = jnp.exp(-pole_rate)
    pole_gain = residue * jnp.sqrt(2.0 * pole_rate) / 4.0

    def advance(carry_state, inputs):
        carry_state = pole_decay * carry_state + inputs[None, :]
        return (carry_state, lax.optimization_barrier(jnp.sum(pole_gain * carry_state, axis=0)))
    last_state, convolved = lax.scan(advance, start_state, product)
    return (query_part * (convolved + skip_gain * product)).astype(jnp.bfloat16)
```

```python
import functools

import jax
import jax.numpy as jnp
from jax import lax
from jax.experimental import pallas as pl
from jax.experimental.pallas import tpu as pltpu
from jax.sharding import PartitionSpec as P

MESH = pl.DeviceIdType.MESH
SEG = 8
LANES = 128
F32 = jnp.float32


def spread(row):
    return jnp.broadcast_to(row, (SEG, LANES))


def mixer(
    count, per_chunk,
    features, taps, history, rate, residue, skip, start,
    out,
    held, ext, weight, prod, query, inner, decay, seg1, seg2, seg4, whole,
    gain, filt, lift, scanned, send, recv, kv_send, kv_recv, q_send, q_recv, result,
    in_sem, tail_sem, out_sem, state_send, state_recv, halo_send, halo_recv,
):
    parts, tokens, width = held.shape
    margin = taps.shape[1] - 1
    length = tokens // SEG
    columns = width // LANES
    chunks = columns // per_chunk
    span = per_chunk * LANES
    half = width // 2
    poles = rate.shape[0]
    here = lax.axis_index("seq")
    first, last = here == 0, here == count - 1
    onward = lax.rem(here + 1, count)
    back = lax.rem(here + count - 1, count)

    def lanes(c):
        return pl.ds(pl.multiple_of(c * LANES, LANES), LANES)

    def fetch(k):
        area = pl.ds(pl.multiple_of(k * span, span), span)
        return pltpu.make_async_copy(features.at[:, :, area], held.at[:, :, area], in_sem.at[k])

    def put(k):
        area = pl.ds(pl.multiple_of(k * span, span), span)
        return pltpu.make_async_copy(result.at[:, area], out.at[:, area], out_sem.at[k])

    def state_copy(k):
        return pltpu.make_async_remote_copy(
            src_ref=send.at[k], dst_ref=recv.at[k], send_sem=state_send.at[k],
            recv_sem=state_recv.at[k], device_id={"seq": onward}, device_id_type=MESH,
        )

    def halo_copy(src, dst, k):
        return pltpu.make_async_remote_copy(
            src_ref=src, dst_ref=dst, send_sem=halo_send.at[k],
            recv_sem=halo_recv.at[k], device_id={"seq": onward}, device_id_type=MESH,
        )

    kv_copy = halo_copy(kv_send, kv_recv, 0)
    q_copy = halo_copy(q_send, q_recv, 1)

    barrier = pltpu.get_barrier_semaphore()

    @pl.when(jnp.logical_not(first))
    def _():
        pl.semaphore_signal(barrier, inc=1, device_id={"seq": back}, device_id_type=MESH)

    @pl.when(jnp.logical_not(last))
    def _():
        pl.semaphore_signal(barrier, inc=1, device_id={"seq": onward}, device_id_type=MESH)

    for k in range(chunks):
        fetch(k).start()

    rows = lax.broadcasted_iota(jnp.int32, (SEG, LANES), 0)

    def powers(one, two, four):
        value = jnp.where(rows % 2 == 1, one, 1.0)
        value = value * jnp.where((rows // 2) % 2 == 1, two, 1.0)
        return value * jnp.where(rows // 4 == 1, four, 1.0)

    def prepare(c, carry):
        r = rate[:, lanes(c)]
        g = residue[:, lanes(c)] * jnp.sqrt(2.0 * r) / 4.0
        a1 = jnp.exp(-r)
        a2 = jnp.exp(-2.0 * r)
        a4 = jnp.exp(-4.0 * r)
        a8 = jnp.exp(-8.0 * r)
        s1 = jnp.exp(-float(length) * r)
        s2 = jnp.exp(-float(2 * length) * r)
        s4 = jnp.exp(-float(4 * length) * r)
        decay[c] = a1
        gain[c] = g
        seg1[c], seg2[c], seg4[c] = s1, s2, s4
        whole[c] = jnp.exp(-float(tokens) * r)
        block = [jnp.zeros((SEG, LANES), F32) for _ in range(length // SEG)]
        for n in range(poles):
            part = spread(g[n : n + 1]) * powers(
                spread(a1[n : n + 1]), spread(a2[n : n + 1]), spread(a4[n : n + 1])
            )
            up = spread(a8[n : n + 1])
            for b in range(length // SEG):
                block[b] = block[b] + part
                part = part * up
            lift[c, n] = powers(
                spread(s1[n : n + 1]), spread(s2[n : n + 1]), spread(s4[n : n + 1])
            )
        direct = jnp.where(rows == 0, spread(skip[:, lanes(c)]), 0.0)
        block[0] = block[0] + direct
        for b in range(length // SEG):
            filt[c, b * SEG : (b + 1) * SEG] = block[b]
        for j in range(parts):
            weight[c, j * 8 : j * 8 + margin + 1] = taps[j, :, lanes(c)].astype(F32)
        return carry

    for k in range(chunks):
        fetch(k).wait()

    tail = pl.ds(tokens - 16, 16)

    def pack(c, carry):
        k_rows = held[1, tail, lanes(c)].astype(F32)[8:]
        v_rows = held[2, tail, lanes(c)].astype(F32)[8:]
        kv_send[:, lanes(c)] = jnp.concatenate([k_rows, v_rows], axis=0).astype(jnp.bfloat16)
        return carry

    lax.fori_loop(0, columns, pack, 0)

    def pack_q(c, carry):
        low = held[0, tail, lanes(c)].astype(F32)[8:]
        high = held[0, tail, lanes(c + columns // 2)].astype(F32)[8:]
        q_send[:, lanes(c)] = jnp.concatenate([low, high], axis=0).astype(jnp.bfloat16)
        return carry

    lax.fori_loop(0, columns // 2, pack_q, 0)

    peers = jnp.where(first, 0, 1) + jnp.where(last, 0, 1)
    pl.semaphore_wait(barrier, peers)

    @pl.when(jnp.logical_not(last))
    def _():
        kv_copy.start()
        q_copy.start()

    lax.fori_loop(0, columns, prepare, 0)

    def widen(c, carry):
        for j in range(parts):
            ext[j, c, 8 : 8 + tokens] = held[j, :, lanes(c)].astype(F32)
        return carry

    lax.fori_loop(0, columns, widen, 0)

    @pl.when(first)
    def _():
        for i in range(margin):
            row = history[i].astype(F32)
            for j in range(parts):
                for c in range(columns):
                    ext[j, c, 8 - margin + i : 9 - margin + i] = row[
                        j : j + 1, c * LANES : (c + 1) * LANES
                    ]

        def begin(c, carry):
            recv[c // per_chunk, c % per_chunk] = start[:, lanes(c)]
            return carry

        lax.fori_loop(0, columns, begin, 0)

    @pl.when(jnp.logical_not(first))
    def _():
        kv_copy.wait_recv()
        q_copy.wait_recv()

        def unpack(c, carry):
            both = kv_recv[:, lanes(c)].astype(F32)
            ext[1, c, 0:8] = both[:8]
            ext[2, c, 0:8] = both[8:]
            return carry

        lax.fori_loop(0, columns, unpack, 0)

        def unpack_q(c, carry):
            both = q_recv[:, lanes(c)].astype(F32)
            ext[0, c, 0:8] = both[:8]
            ext[0, c + columns // 2, 0:8] = both[8:]
            return carry

        lax.fori_loop(0, columns // 2, unpack_q, 0)

    def filtered(j, c):
        x = [ext[j, c, pl.ds(8 + i, SEG, stride=length), :] for i in range(-margin, length)]
        w = [spread(weight[c, j * 8 + i : j * 8 + i + 1]) for i in range(margin + 1)]
        gained = []
        for t in range(length):
            value = w[0] * x[t + margin]
            for i in range(1, margin + 1):
                value = value + w[i] * x[t + margin - i]
            gained.append(value)
        return gained

    def shifted(value, by):
        return pltpu.roll(value, by, 0)

    def end_states(c, carry):
        left = filtered(1, c)
        right = filtered(2, c)
        p = [u * v for u, v in zip(left, right)]
        for t in range(length):
            prod[c, t] = p[t]
        for n in range(poles):
            a = spread(decay[c, n : n + 1])
            state = p[0]
            for t in range(1, length):
                state = a * state + p[t]
            for by, ref in ((1, seg1), (2, seg2), (4, seg4)):
                step = jnp.where(rows >= by, spread(ref[c, n : n + 1]), 0.0)
                state = state + step * shifted(state, by)
            scanned[c, n * SEG : (n + 1) * SEG] = state
        return carry

    def hand_on(k):
        for m in range(per_chunk):
            c = k * per_chunk + m
            ends = jnp.concatenate(
                [
                    scanned[c, pl.ds(b * 64 + SEG - 1, 8, stride=SEG), :]
                    for b in range(poles // 8)
                ],
                axis=0,
            )
            send[k, m] = whole[c] * recv[k, m] + ends
        state_copy(k).start()

    def first_pass(k, carry):
        lax.fori_loop(k * per_chunk, (k + 1) * per_chunk, end_states, 0)

        @pl.when(jnp.logical_and(first, jnp.logical_not(last)))
        def _():
            hand_on(k)

        return carry

    lax.fori_loop(0, chunks, first_pass, 0)

    def inside(c, carry):
        q = filtered(0, c)
        for t in range(length):
            query[c, t] = q[t]
        p = [prod[c, t] for t in range(length)]
        h = [spread(filt[c, i : i + 1]) for i in range(length)]
        for t in range(length):
            value = h[0] * p[t]
            for i in range(1, t + 1):
                value = value + h[i] * p[t - i]
            inner[c, t] = value
        return carry

    def second_pass(k, carry):
        @pl.when(jnp.logical_and(jnp.logical_not(first), jnp.logical_not(last)))
        def _():
            state_copy(k).wait_recv()
            hand_on(k)

        lax.fori_loop(k * per_chunk, (k + 1) * per_chunk, inside, 0)
        return carry

    lax.fori_loop(0, chunks, second_pass, 0)

    def correct(c, carry):
        k, m = c // per_chunk, c % per_chunk
        w, a = [], []
        for n in range(poles):
            local = jnp.where(rows >= 1, shifted(scanned[c, n * SEG : (n + 1) * SEG], 1), 0.0)
            state = local + lift[c, n] * spread(recv[k, m, n : n + 1])
            w.append(spread(gain[c, n : n + 1]) * state)
            a.append(spread(decay[c, n : n + 1]))
        for t in range(length):
            w = [u * v for u, v in zip(w, a)]
            terms = list(w)
            while len(terms) > 1:
                terms = [terms[i] + terms[i + 1] for i in range(0, len(terms), 2)]
            value = query[c, t] * (inner[c, t] + terms[0])
            ext[0, c, pl.ds(t, SEG, stride=length), :] = value
        result[:, lanes(c)] = ext[0, c, 0:tokens].astype(jnp.bfloat16)
        return carry

    def third_pass(k, carry):
        @pl.when(jnp.logical_and(last, jnp.logical_not(first)))
        def _():
            state_copy(k).wait_recv()

        lax.fori_loop(k * per_chunk, (k + 1) * per_chunk, correct, 0)
        put(k).start()
        return carry

    lax.fori_loop(0, chunks, third_pass, 0)

    @pl.when(jnp.logical_not(last))
    def _():
        kv_copy.wait_send()
        q_copy.wait_send()
        for k in range(chunks):
            state_copy(k).wait_send()

    for k in range(chunks):
        put(k).wait()


def body(features, conv_weight, history, pole_rate, residue, skip_gain, start_state):
    tokens, parts, width = features.shape
    poles = pole_rate.shape[0]
    columns = width // LANES
    per_chunk = 2
    chunks = columns // per_chunk
    length = tokens // SEG
    count = lax.axis_size("seq")
    vmem = pl.BlockSpec(memory_space=pltpu.VMEM)
    hbm = pl.BlockSpec(memory_space=pl.ANY)
    small = pltpu.VMEM((columns, poles, LANES), F32)
    dma = pltpu.SemaphoreType.DMA
    return pl.pallas_call(
        functools.partial(mixer, count, per_chunk),
        out_shape=jax.ShapeDtypeStruct((tokens, width), jnp.bfloat16),
        in_specs=[hbm] + [vmem] * 6,
        out_specs=hbm,
        scratch_shapes=[
            pltpu.VMEM((parts, tokens, width), jnp.bfloat16),
            pltpu.VMEM((parts, columns, tokens + 8, LANES), F32),
            pltpu.VMEM((columns, 8 * parts, LANES), F32),
            pltpu.VMEM((columns, length, SEG, LANES), F32),
            pltpu.VMEM((columns, length, SEG, LANES), F32),
            pltpu.VMEM((columns, length, SEG, LANES), F32),
            small, small, small, small, small, small,
            pltpu.VMEM((columns, length, LANES), F32),
            pltpu.VMEM((columns, poles, SEG, LANES), F32),
            pltpu.VMEM((columns, poles * SEG, LANES), F32),
            pltpu.VMEM((chunks, per_chunk, poles, LANES), F32),
            pltpu.VMEM((chunks, per_chunk, poles, LANES), F32),
            pltpu.VMEM((16, width), jnp.bfloat16),
            pltpu.VMEM((16, width), jnp.bfloat16),
            pltpu.VMEM((16, width // 2), jnp.bfloat16),
            pltpu.VMEM((16, width // 2), jnp.bfloat16),
            pltpu.VMEM((tokens, width), jnp.bfloat16),
            dma((chunks,)), dma((1,)), dma((chunks,)), dma((chunks,)), dma((chunks,)),
            dma((2,)), dma((2,)),
        ],
        compiler_params=pltpu.CompilerParams(
            collective_id=0, has_side_effects=True, vmem_limit_bytes=40 * 1024 * 1024
        ),
    )(
        features.transpose(1, 0, 2), conv_weight.transpose(1, 0, 2), history,
        pole_rate, residue, skip_gain[None], start_state,
    )


def solution(mesh):
    return jax.shard_map(
        body,
        mesh=mesh,
        in_specs=(
            P(("grp", "seq"), None, "chan"),
            P(None, None, "chan"),
            P("grp", None, "chan"),
            P(None, "chan"),
            P(None, "chan"),
            P("chan"),
            P("grp", "chan"),
        ),
        out_specs=P(("grp", "seq"), "chan"),
        check_vma=False,
    )
```

```python
import functools

import jax
import jax.numpy as jnp
from jax import lax
from jax.experimental import pallas as pl
from jax.experimental.pallas import tpu as pltpu
from jax.sharding import PartitionSpec as P

MESH = pl.DeviceIdType.MESH
SEG = 8
LANES = 128
F32 = jnp.float32


def spread(row):
    return jnp.broadcast_to(row, (SEG, LANES))


def mixer(
    count, per_chunk,
    features, taps_in, history_in, rate_in, residue_in, skip_in, start_in,
    out,
    taps, history, rate, residue, skip, start, ends_here, held, ext, weight, prod, query, inner, decay, seg1, seg2, seg4, whole,
    gain, filt, lift, scanned, send, recv, kv_send, kv_recv, q_send, q_recv, result,
    in_sem, own_sem, out_sem, state_send, state_recv, halo_send, halo_recv,
):
    parts, tokens, width = held.shape
    margin = taps.shape[1] - 1
    length = tokens // SEG
    columns = width // LANES
    chunks = columns // per_chunk
    span = per_chunk * LANES
    half = width // 2
    poles = rate.shape[0]
    here = lax.axis_index("seq")
    first, last = here == 0, here == count - 1
    onward = lax.rem(here + 1, count)
    back = lax.rem(here + count - 1, count)

    def lanes(c):
        return pl.ds(pl.multiple_of(c * LANES, LANES), LANES)

    def fetch(k):
        area = pl.ds(pl.multiple_of(k * span, span), span)
        return pltpu.make_async_copy(features.at[:, :, area], held.at[:, :, area], in_sem.at[k])

    def put(k):
        area = pl.ds(pl.multiple_of(k * span, span), span)
        return pltpu.make_async_copy(result.at[:, area], out.at[:, area], out_sem.at[k])

    def state_copy(k):
        return pltpu.make_async_remote_copy(
            src_ref=send.at[k], dst_ref=recv.at[k], send_sem=state_send.at[k],
            recv_sem=state_recv.at[k], device_id={"seq": onward}, device_id_type=MESH,
        )

    def halo_copy(src, dst, k):
        return pltpu.make_async_remote_copy(
            src_ref=src, dst_ref=dst, send_sem=halo_send.at[k],
            recv_sem=halo_recv.at[k], device_id={"seq": onward}, device_id_type=MESH,
        )

    kv_copy = halo_copy(kv_send, kv_recv, 0)
    q_copy = halo_copy(q_send, q_recv, 1)

    barrier = pltpu.get_barrier_semaphore()

    @pl.when(jnp.logical_not(first))
    def _():
        pl.semaphore_signal(barrier, inc=1, device_id={"seq": back}, device_id_type=MESH)

    @pl.when(jnp.logical_not(last))
    def _():
        pl.semaphore_signal(barrier, inc=1, device_id={"seq": onward}, device_id_type=MESH)

    tail = pl.ds(tokens - 16, 16)
    owned = [
        pltpu.make_async_copy(src, dst, own_sem.at[i])
        for i, (src, dst) in enumerate(
            (
                (features.at[:, tail], ends_here),
                (rate_in, rate),
                (residue_in, residue),
                (skip_in, skip),
                (taps_in, taps),
                (start_in, start),
                (history_in, history),
            )
        )
    ]
    for copy in owned:
        copy.start()
    for k in range(chunks):
        fetch(k).start()

    rows = lax.broadcasted_iota(jnp.int32, (SEG, LANES), 0)

    def powers(one, two, four):
        value = jnp.where(rows % 2 == 1, one, 1.0)
        value = value * jnp.where((rows // 2) % 2 == 1, two, 1.0)
        return value * jnp.where(rows // 4 == 1, four, 1.0)

    def prepare(c, carry):
        r = rate[:, lanes(c)]
        g = residue[:, lanes(c)] * jnp.sqrt(2.0 * r) / 4.0
        a1 = jnp.exp(-r)
        a2 = jnp.exp(-2.0 * r)
        a4 = jnp.exp(-4.0 * r)
        a8 = jnp.exp(-8.0 * r)
        s1 = jnp.exp(-float(length) * r)
        s2 = jnp.exp(-float(2 * length) * r)
        s4 = jnp.exp(-float(4 * length) * r)
        decay[c] = a1
        gain[c] = g
        seg1[c], seg2[c], seg4[c] = s1, s2, s4
        whole[c] = jnp.exp(-float(tokens) * r)
        block = [jnp.zeros((SEG, LANES), F32) for _ in range(length // SEG)]
        for n in range(poles):
            part = spread(g[n : n + 1]) * powers(
                spread(a1[n : n + 1]), spread(a2[n : n + 1]), spread(a4[n : n + 1])
            )
            up = spread(a8[n : n + 1])
            for b in range(length // SEG):
                block[b] = block[b] + part
                part = part * up
            lift[c, n] = powers(
                spread(s1[n : n + 1]), spread(s2[n : n + 1]), spread(s4[n : n + 1])
            )
        direct = jnp.where(rows == 0, spread(skip[:, lanes(c)]), 0.0)
        block[0] = block[0] + direct
        for b in range(length // SEG):
            filt[c, b * SEG : (b + 1) * SEG] = block[b]
        for j in range(parts):
            weight[c, j * 8 : j * 8 + margin + 1] = taps[j, :, lanes(c)].astype(F32)
        return carry

    owned[0].wait()

    def pack(c, carry):
        k_rows = ends_here[1, :, lanes(c)].astype(F32)[8:]
        v_rows = ends_here[2, :, lanes(c)].astype(F32)[8:]
        kv_send[:, lanes(c)] = jnp.concatenate([k_rows, v_rows], axis=0).astype(jnp.bfloat16)
        return carry

    lax.fori_loop(0, columns, pack, 0)

    def pack_q(c, carry):
        low = ends_here[0, :, lanes(c)].astype(F32)[8:]
        high = ends_here[0, :, lanes(c + columns // 2)].astype(F32)[8:]
        q_send[:, lanes(c)] = jnp.concatenate([low, high], axis=0).astype(jnp.bfloat16)
        return carry

    lax.fori_loop(0, columns // 2, pack_q, 0)

    peers = jnp.where(first, 0, 1) + jnp.where(last, 0, 1)
    pl.semaphore_wait(barrier, peers)

    @pl.when(jnp.logical_not(last))
    def _():
        kv_copy.start()
        q_copy.start()

    for copy in owned[1:]:
        copy.wait()
    lax.fori_loop(0, columns, prepare, 0)

    def widen(c, carry):
        for j in range(parts):
            ext[j, c, 8 : 8 + tokens] = held[j, :, lanes(c)].astype(F32)
        return carry

    def widen_chunk(k, carry):
        fetch(k).wait()
        lax.fori_loop(k * per_chunk, (k + 1) * per_chunk, widen, 0)
        return carry

    lax.fori_loop(0, chunks, widen_chunk, 0)

    @pl.when(first)
    def _():
        for i in range(margin):
            row = history[i].astype(F32)
            for j in range(parts):
                for c in range(columns):
                    ext[j, c, 8 - margin + i : 9 - margin + i] = row[
                        j : j + 1, c * LANES : (c + 1) * LANES
                    ]

        def begin(c, carry):
            recv[c // per_chunk, c % per_chunk] = start[:, lanes(c)]
            return carry

        lax.fori_loop(0, columns, begin, 0)

    @pl.when(jnp.logical_not(first))
    def _():
        kv_copy.wait_recv()
        q_copy.wait_recv()

        def unpack(c, carry):
            both = kv_recv[:, lanes(c)].astype(F32)
            ext[1, c, 0:8] = both[:8]
            ext[2, c, 0:8] = both[8:]
            return carry

        lax.fori_loop(0, columns, unpack, 0)

        def unpack_q(c, carry):
            both = q_recv[:, lanes(c)].astype(F32)
            ext[0, c, 0:8] = both[:8]
            ext[0, c + columns // 2, 0:8] = both[8:]
            return carry

        lax.fori_loop(0, columns // 2, unpack_q, 0)

    def filtered(j, c):
        x = [ext[j, c, pl.ds(8 + i, SEG, stride=length), :] for i in range(-margin, length)]
        w = [spread(weight[c, j * 8 + i : j * 8 + i + 1]) for i in range(margin + 1)]
        gained = []
        for t in range(length):
            value = w[0] * x[t + margin]
            for i in range(1, margin + 1):
                value = value + w[i] * x[t + margin - i]
            gained.append(value)
        return gained

    def shifted(value, by):
        return pltpu.roll(value, by, 0)

    def end_states(c, carry):
        left = filtered(1, c)
        right = filtered(2, c)
        p = [u * v for u, v in zip(left, right)]
        for t in range(length):
            prod[c, t] = p[t]
        for n in range(poles):
            a = spread(decay[c, n : n + 1])
            state = p[0]
            for t in range(1, length):
                state = a * state + p[t]
            for by, ref in ((1, seg1), (2, seg2), (4, seg4)):
                step = jnp.where(rows >= by, spread(ref[c, n : n + 1]), 0.0)
                state = state + step * shifted(state, by)
            scanned[c, n * SEG : (n + 1) * SEG] = state
        return carry

    def hand_on(k):
        for m in range(per_chunk):
            c = k * per_chunk + m
            ends = jnp.concatenate(
                [
                    scanned[c, pl.ds(b * 64 + SEG - 1, 8, stride=SEG), :]
                    for b in range(poles // 8)
                ],
                axis=0,
            )
            send[k, m] = whole[c] * recv[k, m] + ends
        state_copy(k).start()

    def first_pass(k, carry):
        lax.fori_loop(k * per_chunk, (k + 1) * per_chunk, end_states, 0)

        @pl.when(jnp.logical_and(first, jnp.logical_not(last)))
        def _():
            hand_on(k)

        @pl.when(jnp.logical_and(here == 1, jnp.logical_not(last)))
        def _():
            state_copy(k).wait_recv()
            hand_on(k)

        return carry

    lax.fori_loop(0, chunks, first_pass, 0)

    def inside(c, carry):
        q = filtered(0, c)
        for t in range(length):
            query[c, t] = q[t]
        p = [prod[c, t] for t in range(length)]
        h = [spread(filt[c, i : i + 1]) for i in range(length)]
        for t in range(length):
            value = h[0] * p[t]
            for i in range(1, t + 1):
                value = value + h[i] * p[t - i]
            inner[c, t] = value
        return carry

    def second_pass(k, carry):
        @pl.when(jnp.logical_and(here > 1, jnp.logical_not(last)))
        def _():
            state_copy(k).wait_recv()
            hand_on(k)

        lax.fori_loop(k * per_chunk, (k + 1) * per_chunk, inside, 0)
        return carry

    lax.fori_loop(0, chunks, second_pass, 0)

    def correct(c, carry):
        k, m = c // per_chunk, c % per_chunk
        w, a = [], []
        for n in range(poles):
            local = jnp.where(rows >= 1, shifted(scanned[c, n * SEG : (n + 1) * SEG], 1), 0.0)
            state = local + lift[c, n] * spread(recv[k, m, n : n + 1])
            w.append(spread(gain[c, n : n + 1]) * state)
            a.append(spread(decay[c, n : n + 1]))
        for t in range(length):
            w = [u * v for u, v in zip(w, a)]
            terms = list(w)
            while len(terms) > 1:
                terms = [terms[i] + terms[i + 1] for i in range(0, len(terms), 2)]
            value = query[c, t] * (inner[c, t] + terms[0])
            ext[0, c, pl.ds(t, SEG, stride=length), :] = value
        result[:, lanes(c)] = ext[0, c, 0:tokens].astype(jnp.bfloat16)
        return carry

    def third_pass(k, carry):
        @pl.when(jnp.logical_and(last, jnp.logical_not(first)))
        def _():
            state_copy(k).wait_recv()

        lax.fori_loop(k * per_chunk, (k + 1) * per_chunk, correct, 0)
        put(k).start()
        return carry

    lax.fori_loop(0, chunks, third_pass, 0)

    @pl.when(jnp.logical_not(last))
    def _():
        kv_copy.wait_send()
        q_copy.wait_send()
        for k in range(chunks):
            state_copy(k).wait_send()

    for k in range(chunks):
        put(k).wait()


def body(features, conv_weight, history, pole_rate, residue, skip_gain, start_state):
    tokens, parts, width = features.shape
    poles = pole_rate.shape[0]
    columns = width // LANES
    per_chunk = 2
    chunks = columns // per_chunk
    length = tokens // SEG
    count = lax.axis_size("seq")
    hbm = pl.BlockSpec(memory_space=pltpu.HBM)
    small = pltpu.VMEM((columns, poles, LANES), F32)
    dma = pltpu.SemaphoreType.DMA
    return pl.pallas_call(
        functools.partial(mixer, count, per_chunk),
        out_shape=jax.ShapeDtypeStruct((tokens, width), jnp.bfloat16),
        in_specs=[hbm] * 7,
        out_specs=hbm,
        scratch_shapes=[
            pltpu.VMEM((parts,) + conv_weight.shape[:1] + (width,), jnp.bfloat16),
            pltpu.VMEM(history.shape, jnp.bfloat16),
            pltpu.VMEM((poles, width), F32),
            pltpu.VMEM((poles, width), F32),
            pltpu.VMEM((1, width), F32),
            pltpu.VMEM((poles, width), F32),
            pltpu.VMEM((parts, 16, width), jnp.bfloat16),
            pltpu.VMEM((parts, tokens, width), jnp.bfloat16),
            pltpu.VMEM((parts, columns, tokens + 8, LANES), F32),
            pltpu.VMEM((columns, 8 * parts, LANES), F32),
            pltpu.VMEM((columns, length, SEG, LANES), F32),
            pltpu.VMEM((columns, length, SEG, LANES), F32),
            pltpu.VMEM((columns, length, SEG, LANES), F32),
            small, small, small, small, small, small,
            pltpu.VMEM((columns, length, LANES), F32),
            pltpu.VMEM((columns, poles, SEG, LANES), F32),
            pltpu.VMEM((columns, poles * SEG, LANES), F32),
            pltpu.VMEM((chunks, per_chunk, poles, LANES), F32),
            pltpu.VMEM((chunks, per_chunk, poles, LANES), F32),
            pltpu.VMEM((16, width), jnp.bfloat16),
            pltpu.VMEM((16, width), jnp.bfloat16),
            pltpu.VMEM((16, width // 2), jnp.bfloat16),
            pltpu.VMEM((16, width // 2), jnp.bfloat16),
            pltpu.VMEM((tokens, width), jnp.bfloat16),
            dma((chunks,)), dma((7,)), dma((chunks,)), dma((chunks,)), dma((chunks,)),
            dma((2,)), dma((2,)),
        ],
        compiler_params=pltpu.CompilerParams(
            collective_id=0, has_side_effects=True, vmem_limit_bytes=60 * 1024 * 1024
        ),
    )(
        features.transpose(1, 0, 2), conv_weight.transpose(1, 0, 2), history,
        pole_rate, residue, skip_gain[None], start_state,
    )


def solution(mesh):
    return jax.shard_map(
        body,
        mesh=mesh,
        in_specs=(
            P(("grp", "seq"), None, "chan"),
            P(None, None, "chan"),
            P("grp", None, "chan"),
            P(None, "chan"),
            P(None, "chan"),
            P("chan"),
            P("grp", "chan"),
        ),
        out_specs=P(("grp", "seq"), "chan"),
        check_vma=False,
    )
```

```python
import functools

import jax
import jax.numpy as jnp
from jax import lax
from jax.experimental import pallas as pl
from jax.experimental.pallas import tpu as pltpu
from jax.sharding import PartitionSpec as P

MESH = pl.DeviceIdType.MESH
SEG = 8
LANES = 128
F32 = jnp.float32


def spread(row):
    return jnp.broadcast_to(row, (SEG, LANES))


def mixer(
    count, per_chunk,
    features, taps_in, history_in, rate_in, residue_in, skip_in, start_in,
    out,
    taps, history, rate, residue, skip, start, ends_here, held, ext, weight, prod, query, inner, decay, rest, seg1, seg2, seg4, whole,
    gain, filt, lift, scanned, send, recv, kv_send, kv_recv, q_send, q_recv, result,
    in_sem, own_sem, out_sem, state_send, state_recv, halo_send, halo_recv,
):
    parts, tokens, width = held.shape
    margin = taps.shape[1] - 1
    length = tokens // SEG
    columns = width // LANES
    chunks = columns // per_chunk
    span = per_chunk * LANES
    half = width // 2
    poles = rate.shape[0]
    here = lax.axis_index("seq")
    first, last = here == 0, here == count - 1
    onward = lax.rem(here + 1, count)
    back = lax.rem(here + count - 1, count)

    def lanes(c):
        return pl.ds(pl.multiple_of(c * LANES, LANES), LANES)

    def fetch(k):
        area = pl.ds(pl.multiple_of(k * span, span), span)
        return pltpu.make_async_copy(features.at[:, :, area], held.at[:, :, area], in_sem.at[k])

    def put(k):
        area = pl.ds(pl.multiple_of(k * span, span), span)
        return pltpu.make_async_copy(result.at[:, area], out.at[:, area], out_sem.at[k])

    def state_copy(k):
        return pltpu.make_async_remote_copy(
            src_ref=send.at[k], dst_ref=recv.at[k], send_sem=state_send.at[k],
            recv_sem=state_recv.at[k], device_id={"seq": onward}, device_id_type=MESH,
        )

    def halo_copy(src, dst, k):
        return pltpu.make_async_remote_copy(
            src_ref=src, dst_ref=dst, send_sem=halo_send.at[k],
            recv_sem=halo_recv.at[k], device_id={"seq": onward}, device_id_type=MESH,
        )

    kv_copy = halo_copy(kv_send, kv_recv, 0)
    q_copy = halo_copy(q_send, q_recv, 1)

    barrier = pltpu.get_barrier_semaphore()

    @pl.when(jnp.logical_not(first))
    def _():
        pl.semaphore_signal(barrier, inc=1, device_id={"seq": back}, device_id_type=MESH)

    @pl.when(jnp.logical_not(last))
    def _():
        pl.semaphore_signal(barrier, inc=1, device_id={"seq": onward}, device_id_type=MESH)

    tail = pl.ds(tokens - 16, 16)
    owned = [
        pltpu.make_async_copy(src, dst, own_sem.at[i])
        for i, (src, dst) in enumerate(
            (
                (features.at[:, tail], ends_here),
                (rate_in, rate),
                (residue_in, residue),
                (skip_in, skip),
                (taps_in, taps),
                (start_in, start),
                (history_in, history),
            )
        )
    ]
    for copy in owned:
        copy.start()
    for k in range(chunks):
        fetch(k).start()

    rows = lax.broadcasted_iota(jnp.int32, (SEG, LANES), 0)

    def powers(one, two, four):
        value = jnp.where(rows % 2 == 1, one, 1.0)
        value = value * jnp.where((rows // 2) % 2 == 1, two, 1.0)
        return value * jnp.where(rows // 4 == 1, four, 1.0)

    def prepare(c, carry):
        r = rate[:, lanes(c)]
        decay[c] = jnp.exp(-r)
        rest[c] = jnp.exp(-float(length - margin) * r)
        seg1[c] = jnp.exp(-float(length) * r)
        seg2[c] = jnp.exp(-float(2 * length) * r)
        seg4[c] = jnp.exp(-float(4 * length) * r)
        whole[c] = jnp.exp(-float(tokens) * r)
        for j in range(parts):
            weight[c, j * 8 : j * 8 + margin + 1] = taps[j, :, lanes(c)].astype(F32)
        return carry

    def prepare_more(c, carry):
        r = rate[:, lanes(c)]
        g = residue[:, lanes(c)] * jnp.sqrt(2.0 * r) / 4.0
        a1 = decay[c]
        a2 = jnp.exp(-2.0 * r)
        a4 = jnp.exp(-4.0 * r)
        a8 = jnp.exp(-8.0 * r)
        s1, s2, s4 = seg1[c], seg2[c], seg4[c]
        gain[c] = g
        block = [jnp.zeros((SEG, LANES), F32) for _ in range(length // SEG)]
        for n in range(poles):
            part = spread(g[n : n + 1]) * powers(
                spread(a1[n : n + 1]), spread(a2[n : n + 1]), spread(a4[n : n + 1])
            )
            up = spread(a8[n : n + 1])
            for b in range(length // SEG):
                block[b] = block[b] + part
                part = part * up
            lift[c, n] = powers(
                spread(s1[n : n + 1]), spread(s2[n : n + 1]), spread(s4[n : n + 1])
            )
        direct = jnp.where(rows == 0, spread(skip[:, lanes(c)]), 0.0)
        block[0] = block[0] + direct
        for b in range(length // SEG):
            filt[c, b * SEG : (b + 1) * SEG] = block[b]
        return carry

    owned[0].wait()

    def pack(c, carry):
        k_rows = ends_here[1, :, lanes(c)].astype(F32)[8:]
        v_rows = ends_here[2, :, lanes(c)].astype(F32)[8:]
        kv_send[:, lanes(c)] = jnp.concatenate([k_rows, v_rows], axis=0).astype(jnp.bfloat16)
        return carry

    lax.fori_loop(0, columns, pack, 0)

    def pack_q(c, carry):
        low = ends_here[0, :, lanes(c)].astype(F32)[8:]
        high = ends_here[0, :, lanes(c + columns // 2)].astype(F32)[8:]
        q_send[:, lanes(c)] = jnp.concatenate([low, high], axis=0).astype(jnp.bfloat16)
        return carry

    lax.fori_loop(0, columns // 2, pack_q, 0)

    peers = jnp.where(first, 0, 1) + jnp.where(last, 0, 1)
    pl.semaphore_wait(barrier, peers)

    @pl.when(jnp.logical_not(last))
    def _():
        kv_copy.start()
        q_copy.start()

    def filtered(j, c, low, high):
        x = [ext[j, c, pl.ds(8 + i, SEG, stride=length), :] for i in range(low - margin, high)]
        w = [spread(weight[c, j * 8 + i : j * 8 + i + 1]) for i in range(margin + 1)]
        gained = []
        for t in range(high - low):
            value = w[0] * x[t + margin]
            for i in range(1, margin + 1):
                value = value + w[i] * x[t + margin - i]
            gained.append(value)
        return gained

    def product(c, low, high):
        p = [u * v for u, v in zip(filtered(1, c, low, high), filtered(2, c, low, high))]
        for t in range(low, high):
            prod[c, t] = p[t - low]
        return p

    def summed(c, n, p):
        a = spread(decay[c, n : n + 1])
        state = p[0]
        for value in p[1:]:
            state = a * state + value
        return state

    def shifted(value, by):
        return pltpu.roll(value, by, 0)

    def scan_segments(c, n, state):
        for by, ref in ((1, seg1), (2, seg2), (4, seg4)):
            step = jnp.where(rows >= by, spread(ref[c, n : n + 1]), 0.0)
            state = state + step * shifted(state, by)
        scanned[c, n * SEG : (n + 1) * SEG] = state

    def end_states(c, carry):
        p = product(c, 0, length)
        for n in range(poles):
            scan_segments(c, n, summed(c, n, p))
        return carry

    def end_states_early(c, carry):
        p = product(c, margin, length)
        for n in range(poles):
            scanned[c, n * SEG : (n + 1) * SEG] = summed(c, n, p)
        return carry

    def end_states_late(c, carry):
        p = product(c, 0, margin)
        for n in range(poles):
            early = scanned[c, n * SEG : (n + 1) * SEG]
            scan_segments(c, n, early + spread(rest[c, n : n + 1]) * summed(c, n, p))
        return carry

    def hand_on(k):
        for m in range(per_chunk):
            c = k * per_chunk + m
            ends = jnp.concatenate(
                [
                    scanned[c, pl.ds(b * 64 + SEG - 1, 8, stride=SEG), :]
                    for b in range(poles // 8)
                ],
                axis=0,
            )
            send[k, m] = whole[c] * recv[k, m] + ends
        state_copy(k).start()

    for copy in owned[1:]:
        copy.wait()
    lax.fori_loop(0, columns, prepare, 0)

    def widen(c, carry):
        for j in range(parts):
            ext[j, c, 8 : 8 + tokens] = held[j, :, lanes(c)].astype(F32)
        return carry

    def each(k, step):
        lax.fori_loop(k * per_chunk, (k + 1) * per_chunk, step, 0)

    @pl.when(first)
    def _():
        for i in range(margin):
            row = history[i].astype(F32)
            for j in range(parts):
                for c in range(columns):
                    ext[j, c, 8 - margin + i : 9 - margin + i] = row[
                        j : j + 1, c * LANES : (c + 1) * LANES
                    ]

        def begin(c, carry):
            recv[c // per_chunk, c % per_chunk] = start[:, lanes(c)]
            return carry

        lax.fori_loop(0, columns, begin, 0)

        def only_pass(k, carry):
            fetch(k).wait()
            each(k, widen)
            each(k, end_states)

            @pl.when(jnp.logical_not(last))
            def _():
                hand_on(k)

            return carry

        lax.fori_loop(0, chunks, only_pass, 0)

    @pl.when(jnp.logical_not(first))
    def _():
        def early_pass(k, carry):
            fetch(k).wait()
            each(k, widen)
            each(k, end_states_early)
            return carry

        lax.fori_loop(0, chunks, early_pass, 0)
        kv_copy.wait_recv()
        q_copy.wait_recv()

        def unpack(c, carry):
            both = kv_recv[:, lanes(c)].astype(F32)
            ext[1, c, 0:8] = both[:8]
            ext[2, c, 0:8] = both[8:]
            return carry

        lax.fori_loop(0, columns, unpack, 0)

        def unpack_q(c, carry):
            both = q_recv[:, lanes(c)].astype(F32)
            ext[0, c, 0:8] = both[:8]
            ext[0, c + columns // 2, 0:8] = both[8:]
            return carry

        lax.fori_loop(0, columns // 2, unpack_q, 0)

        def late_pass(k, carry):
            each(k, end_states_late)

            @pl.when(jnp.logical_and(here == 1, jnp.logical_not(last)))
            def _():
                state_copy(k).wait_recv()
                hand_on(k)

            return carry

        lax.fori_loop(0, chunks, late_pass, 0)

    def inside(c, carry):
        q = filtered(0, c, 0, length)
        for t in range(length):
            query[c, t] = q[t]
        p = [prod[c, t] for t in range(length)]
        h = [spread(filt[c, i : i + 1]) for i in range(length)]
        for t in range(length):
            value = h[0] * p[t]
            for i in range(1, t + 1):
                value = value + h[i] * p[t - i]
            inner[c, t] = value
        return carry

    def second_pass(k, carry):
        @pl.when(jnp.logical_and(here > 1, jnp.logical_not(last)))
        def _():
            state_copy(k).wait_recv()
            hand_on(k)

        each(k, prepare_more)
        each(k, inside)
        return carry

    lax.fori_loop(0, chunks, second_pass, 0)

    def correct(c, carry):
        k, m = c // per_chunk, c % per_chunk
        w, a = [], []
        for n in range(poles):
            local = jnp.where(rows >= 1, shifted(scanned[c, n * SEG : (n + 1) * SEG], 1), 0.0)
            state = local + lift[c, n] * spread(recv[k, m, n : n + 1])
            w.append(spread(gain[c, n : n + 1]) * state)
            a.append(spread(decay[c, n : n + 1]))
        for t in range(length):
            w = [u * v for u, v in zip(w, a)]
            terms = list(w)
            while len(terms) > 1:
                terms = [terms[i] + terms[i + 1] for i in range(0, len(terms), 2)]
            value = query[c, t] * (inner[c, t] + terms[0])
            ext[0, c, pl.ds(t, SEG, stride=length), :] = value
        result[:, lanes(c)] = ext[0, c, 0:tokens].astype(jnp.bfloat16)
        return carry

    def third_pass(k, carry):
        @pl.when(jnp.logical_and(last, jnp.logical_not(first)))
        def _():
            state_copy(k).wait_recv()

        each(k, correct)
        put(k).start()
        return carry

    lax.fori_loop(0, chunks, third_pass, 0)

    @pl.when(jnp.logical_not(last))
    def _():
        kv_copy.wait_send()
        q_copy.wait_send()
        for k in range(chunks):
            state_copy(k).wait_send()

    for k in range(chunks):
        put(k).wait()


def settle(parts, source, out, sem):
    rows = source.shape[0] // parts
    copies = [
        pltpu.make_async_copy(
            source.at[pl.ds(i * rows, rows)], out.at[pl.ds(i * rows, rows)], sem.at[i]
        )
        for i in range(parts)
    ]
    for copy in copies:
        copy.start()
    for copy in copies:
        copy.wait()


def body(features, conv_weight, history, pole_rate, residue, skip_gain, start_state):
    tokens, parts, width = features.shape
    poles = pole_rate.shape[0]
    columns = width // LANES
    per_chunk = 2
    chunks = columns // per_chunk
    length = tokens // SEG
    count = lax.axis_size("seq")
    hbm = pl.BlockSpec(memory_space=pltpu.HBM)
    small = pltpu.VMEM((columns, poles, LANES), F32)
    dma = pltpu.SemaphoreType.DMA
    mixed = pl.pallas_call(
        functools.partial(mixer, count, per_chunk),
        out_shape=jax.ShapeDtypeStruct((tokens, width), jnp.bfloat16),
        in_specs=[hbm] * 7,
        out_specs=hbm,
        scratch_shapes=[
            pltpu.VMEM((parts,) + conv_weight.shape[:1] + (width,), jnp.bfloat16),
            pltpu.VMEM(history.shape, jnp.bfloat16),
            pltpu.VMEM((poles, width), F32),
            pltpu.VMEM((poles, width), F32),
            pltpu.VMEM((1, width), F32),
            pltpu.VMEM((poles, width), F32),
            pltpu.VMEM((parts, 16, width), jnp.bfloat16),
            pltpu.VMEM((parts, tokens, width), jnp.bfloat16),
            pltpu.VMEM((parts, columns, tokens + 8, LANES), F32),
            pltpu.VMEM((columns, 8 * parts, LANES), F32),
            pltpu.VMEM((columns, length, SEG, LANES), F32),
            pltpu.VMEM((columns, length, SEG, LANES), F32),
            pltpu.VMEM((columns, length, SEG, LANES), F32),
            small, small, small, small, small, small, small,
            pltpu.VMEM((columns, length, LANES), F32),
            pltpu.VMEM((columns, poles, SEG, LANES), F32),
            pltpu.VMEM((columns, poles * SEG, LANES), F32),
            pltpu.VMEM((chunks, per_chunk, poles, LANES), F32),
            pltpu.VMEM((chunks, per_chunk, poles, LANES), F32),
            pltpu.VMEM((16, width), jnp.bfloat16),
            pltpu.VMEM((16, width), jnp.bfloat16),
            pltpu.VMEM((16, width // 2), jnp.bfloat16),
            pltpu.VMEM((16, width // 2), jnp.bfloat16),
            pltpu.VMEM((tokens, width), jnp.bfloat16),
            dma((chunks,)), dma((7,)), dma((chunks,)), dma((chunks,)), dma((chunks,)),
            dma((2,)), dma((2,)),
        ],
        compiler_params=pltpu.CompilerParams(
            collective_id=0, has_side_effects=True, vmem_limit_bytes=60 * 1024 * 1024
        ),
    )(
        features.transpose(1, 0, 2), conv_weight.transpose(1, 0, 2), history,
        pole_rate, residue, skip_gain[None], start_state,
    )
    pieces = tokens // 16
    return pl.pallas_call(
        functools.partial(settle, pieces),
        out_shape=jax.ShapeDtypeStruct((tokens, width), jnp.bfloat16),
        in_specs=[hbm],
        out_specs=hbm,
        scratch_shapes=[dma((pieces,))],
    )(mixed)


def solution(mesh):
    return jax.shard_map(
        body,
        mesh=mesh,
        in_specs=(
            P(("grp", "seq"), None, "chan"),
            P(None, None, "chan"),
            P("grp", None, "chan"),
            P(None, "chan"),
            P(None, "chan"),
            P("chan"),
            P("grp", "chan"),
        ),
        out_specs=P(("grp", "seq"), "chan"),
        check_vma=False,
    )
```

```python
import functools

import jax
import jax.numpy as jnp
from jax import lax
from jax.experimental import pallas as pl
from jax.experimental.pallas import tpu as pltpu
from jax.sharding import PartitionSpec as P

MESH = pl.DeviceIdType.MESH
SEG = 8
LANES = 128
F32 = jnp.float32


def spread(row):
    return jnp.broadcast_to(row, (SEG, LANES))


def mixer(
    count, per_chunk,
    features, taps_in, history_in, rate_in, residue_in, skip_in, start_in,
    out,
    taps, history, rate, residue, skip, start, ends_here, held, ext, weight, prod, query, inner, decay, rest, seg1, seg2, seg4, whole,
    gain, filt, lift, scanned, send, recv, kv_send, kv_recv, q_send, q_recv,
    in_sem, own_sem, state_send, state_recv, halo_send, halo_recv,
):
    parts, tokens, width = held.shape
    margin = taps.shape[1] - 1
    length = tokens // SEG
    columns = width // LANES
    chunks = columns // per_chunk
    span = per_chunk * LANES
    half = width // 2
    poles = rate.shape[0]
    here = lax.axis_index("seq")
    first, last = here == 0, here == count - 1
    onward = lax.rem(here + 1, count)
    back = lax.rem(here + count - 1, count)

    def lanes(c):
        return pl.ds(pl.multiple_of(c * LANES, LANES), LANES)

    def fetch(k):
        area = pl.ds(pl.multiple_of(k * span, span), span)
        return pltpu.make_async_copy(features.at[:, :, area], held.at[:, :, area], in_sem.at[k])

    def state_copy(k):
        return pltpu.make_async_remote_copy(
            src_ref=send.at[k], dst_ref=recv.at[k], send_sem=state_send.at[k],
            recv_sem=state_recv.at[k], device_id={"seq": onward}, device_id_type=MESH,
        )

    def halo_copy(src, dst, k):
        return pltpu.make_async_remote_copy(
            src_ref=src, dst_ref=dst, send_sem=halo_send.at[k],
            recv_sem=halo_recv.at[k], device_id={"seq": onward}, device_id_type=MESH,
        )

    kv_copy = halo_copy(kv_send, kv_recv, 0)
    q_copy = halo_copy(q_send, q_recv, 1)

    barrier = pltpu.get_barrier_semaphore()

    @pl.when(jnp.logical_not(first))
    def _():
        pl.semaphore_signal(barrier, inc=1, device_id={"seq": back}, device_id_type=MESH)

    @pl.when(jnp.logical_not(last))
    def _():
        pl.semaphore_signal(barrier, inc=1, device_id={"seq": onward}, device_id_type=MESH)

    tail = pl.ds(tokens - 16, 16)
    owned = [
        pltpu.make_async_copy(src, dst, own_sem.at[i])
        for i, (src, dst) in enumerate(
            (
                (features.at[:, tail], ends_here),
                (rate_in, rate),
                (residue_in, residue),
                (skip_in, skip),
                (taps_in, taps),
                (start_in, start),
                (history_in, history),
            )
        )
    ]
    for copy in owned:
        copy.start()
    for k in range(chunks):
        fetch(k).start()

    rows = lax.broadcasted_iota(jnp.int32, (SEG, LANES), 0)

    def powers(one, two, four):
        value = jnp.where(rows % 2 == 1, one, 1.0)
        value = value * jnp.where((rows // 2) % 2 == 1, two, 1.0)
        return value * jnp.where(rows // 4 == 1, four, 1.0)

    def prepare(c, carry):
        r = rate[:, lanes(c)]
        decay[c] = jnp.exp(-r)
        rest[c] = jnp.exp(-float(length - margin) * r)
        seg1[c] = jnp.exp(-float(length) * r)
        seg2[c] = jnp.exp(-float(2 * length) * r)
        seg4[c] = jnp.exp(-float(4 * length) * r)
        whole[c] = jnp.exp(-float(tokens) * r)
        for j in range(parts):
            weight[c, j * 8 : j * 8 + margin + 1] = taps[j, :, lanes(c)].astype(F32)
        return carry

    def prepare_more(c, carry):
        r = rate[:, lanes(c)]
        g = residue[:, lanes(c)] * jnp.sqrt(2.0 * r) / 4.0
        a1 = decay[c]
        a2 = jnp.exp(-2.0 * r)
        a4 = jnp.exp(-4.0 * r)
        a8 = jnp.exp(-8.0 * r)
        s1, s2, s4 = seg1[c], seg2[c], seg4[c]
        gain[c] = g
        block = [jnp.zeros((SEG, LANES), F32) for _ in range(length // SEG)]
        for n in range(poles):
            part = spread(g[n : n + 1]) * powers(
                spread(a1[n : n + 1]), spread(a2[n : n + 1]), spread(a4[n : n + 1])
            )
            up = spread(a8[n : n + 1])
            for b in range(length // SEG):
                block[b] = block[b] + part
                part = part * up
            lift[c, n] = powers(
                spread(s1[n : n + 1]), spread(s2[n : n + 1]), spread(s4[n : n + 1])
            )
        direct = jnp.where(rows == 0, spread(skip[:, lanes(c)]), 0.0)
        block[0] = block[0] + direct
        for b in range(length // SEG):
            filt[c, b * SEG : (b + 1) * SEG] = block[b]
        return carry

    owned[0].wait()

    def pack(c, carry):
        k_rows = ends_here[1, :, lanes(c)].astype(F32)[8:]
        v_rows = ends_here[2, :, lanes(c)].astype(F32)[8:]
        kv_send[:, lanes(c)] = jnp.concatenate([k_rows, v_rows], axis=0).astype(jnp.bfloat16)
        return carry

    lax.fori_loop(0, columns, pack, 0)

    def pack_q(c, carry):
        low = ends_here[0, :, lanes(c)].astype(F32)[8:]
        high = ends_here[0, :, lanes(c + columns // 2)].astype(F32)[8:]
        q_send[:, lanes(c)] = jnp.concatenate([low, high], axis=0).astype(jnp.bfloat16)
        return carry

    lax.fori_loop(0, columns // 2, pack_q, 0)

    peers = jnp.where(first, 0, 1) + jnp.where(last, 0, 1)
    pl.semaphore_wait(barrier, peers)

    @pl.when(jnp.logical_not(last))
    def _():
        kv_copy.start()
        q_copy.start()

    def filtered(j, c, low, high):
        x = [ext[j, c, pl.ds(8 + i, SEG, stride=length), :] for i in range(low - margin, high)]
        w = [spread(weight[c, j * 8 + i : j * 8 + i + 1]) for i in range(margin + 1)]
        gained = []
        for t in range(high - low):
            value = w[0] * x[t + margin]
            for i in range(1, margin + 1):
                value = value + w[i] * x[t + margin - i]
            gained.append(value)
        return gained

    def product(c, low, high):
        p = [u * v for u, v in zip(filtered(1, c, low, high), filtered(2, c, low, high))]
        for t in range(low, high):
            prod[c, t] = p[t - low]
        return p

    def summed(c, n, p):
        a = spread(decay[c, n : n + 1])
        state = p[0]
        for value in p[1:]:
            state = a * state + value
        return state

    def shifted(value, by):
        return pltpu.roll(value, by, 0)

    def scan_segments(c, n, state):
        for by, ref in ((1, seg1), (2, seg2), (4, seg4)):
            step = jnp.where(rows >= by, spread(ref[c, n : n + 1]), 0.0)
            state = state + step * shifted(state, by)
        scanned[c, n * SEG : (n + 1) * SEG] = state

    def end_states(c, carry):
        p = product(c, 0, length)
        for n in range(poles):
            scan_segments(c, n, summed(c, n, p))
        return carry

    def end_states_early(c, carry):
        p = product(c, margin, length)
        for n in range(poles):
            scanned[c, n * SEG : (n + 1) * SEG] = summed(c, n, p)
        return carry

    def end_states_late(c, carry):
        p = product(c, 0, margin)
        for n in range(poles):
            early = scanned[c, n * SEG : (n + 1) * SEG]
            scan_segments(c, n, early + spread(rest[c, n : n + 1]) * summed(c, n, p))
        return carry

    def hand_on(k):
        for m in range(per_chunk):
            c = k * per_chunk + m
            ends = jnp.concatenate(
                [
                    scanned[c, pl.ds(b * 64 + SEG - 1, 8, stride=SEG), :]
                    for b in range(poles // 8)
                ],
                axis=0,
            )
            send[k, m] = whole[c] * recv[k, m] + ends
        state_copy(k).start()

    for copy in owned[1:]:
        copy.wait()
    lax.fori_loop(0, columns, prepare, 0)

    def widen(c, carry):
        for j in range(parts):
            ext[j, c, 8 : 8 + tokens] = held[j, :, lanes(c)].astype(F32)
        return carry

    def each(k, step):
        lax.fori_loop(k * per_chunk, (k + 1) * per_chunk, step, 0)

    @pl.when(first)
    def _():
        def begin(c, carry):
            recv[c // per_chunk, c % per_chunk] = start[:, lanes(c)]
            for i in range(margin):
                row = history[i, :, lanes(c)].astype(F32)
                for j in range(parts):
                    ext[j, c, 8 - margin + i : 9 - margin + i] = row[j : j + 1]
            return carry

        lax.fori_loop(0, columns, begin, 0)

        def only_pass(k, carry):
            fetch(k).wait()
            each(k, widen)
            each(k, end_states)

            @pl.when(jnp.logical_not(last))
            def _():
                hand_on(k)

            return carry

        lax.fori_loop(0, chunks, only_pass, 0)

    @pl.when(jnp.logical_not(first))
    def _():
        def early_pass(k, carry):
            fetch(k).wait()
            each(k, widen)
            each(k, end_states_early)
            return carry

        lax.fori_loop(0, chunks, early_pass, 0)
        kv_copy.wait_recv()
        q_copy.wait_recv()

        def unpack(c, carry):
            both = kv_recv[:, lanes(c)].astype(F32)
            ext[1, c, 0:8] = both[:8]
            ext[2, c, 0:8] = both[8:]
            return carry

        lax.fori_loop(0, columns, unpack, 0)

        def unpack_q(c, carry):
            both = q_recv[:, lanes(c)].astype(F32)
            ext[0, c, 0:8] = both[:8]
            ext[0, c + columns // 2, 0:8] = both[8:]
            return carry

        lax.fori_loop(0, columns // 2, unpack_q, 0)

        def late_pass(k, carry):
            each(k, end_states_late)

            @pl.when(jnp.logical_and(here == 1, jnp.logical_not(last)))
            def _():
                state_copy(k).wait_recv()
                hand_on(k)

            return carry

        lax.fori_loop(0, chunks, late_pass, 0)

    def inside(c, carry):
        q = filtered(0, c, 0, length)
        for t in range(length):
            query[c, t] = q[t]
        p = [prod[c, t] for t in range(length)]
        h = [spread(filt[c, i : i + 1]) for i in range(length)]
        for t in range(length):
            value = h[0] * p[t]
            for i in range(1, t + 1):
                value = value + h[i] * p[t - i]
            inner[c, t] = value
        return carry

    def second_pass(k, carry):
        @pl.when(jnp.logical_and(here > 1, jnp.logical_not(last)))
        def _():
            state_copy(k).wait_recv()
            hand_on(k)

        each(k, prepare_more)
        each(k, inside)
        return carry

    lax.fori_loop(0, chunks, second_pass, 0)

    def correct(c, carry):
        k, m = c // per_chunk, c % per_chunk
        w, a = [], []
        for n in range(poles):
            local = jnp.where(rows >= 1, shifted(scanned[c, n * SEG : (n + 1) * SEG], 1), 0.0)
            state = local + lift[c, n] * spread(recv[k, m, n : n + 1])
            w.append(spread(gain[c, n : n + 1]) * state)
            a.append(spread(decay[c, n : n + 1]))
        for t in range(length):
            w = [u * v for u, v in zip(w, a)]
            terms = list(w)
            while len(terms) > 1:
                terms = [terms[i] + terms[i + 1] for i in range(0, len(terms), 2)]
            value = query[c, t] * (inner[c, t] + terms[0])
            ext[0, c, pl.ds(t, SEG, stride=length), :] = value
        out[:, lanes(c)] = ext[0, c, 0:tokens].astype(jnp.bfloat16)
        return carry

    def third_pass(k, carry):
        @pl.when(jnp.logical_and(last, jnp.logical_not(first)))
        def _():
            state_copy(k).wait_recv()

        each(k, correct)
        return carry

    lax.fori_loop(0, chunks, third_pass, 0)

    @pl.when(jnp.logical_not(last))
    def _():
        kv_copy.wait_send()
        q_copy.wait_send()
        for k in range(chunks):
            state_copy(k).wait_send()


def body(features, conv_weight, history, pole_rate, residue, skip_gain, start_state):
    tokens, parts, width = features.shape
    poles = pole_rate.shape[0]
    columns = width // LANES
    per_chunk = 2
    chunks = columns // per_chunk
    length = tokens // SEG
    count = lax.axis_size("seq")
    hbm = pl.BlockSpec(memory_space=pltpu.HBM)
    small = pltpu.VMEM((columns, poles, LANES), F32)
    dma = pltpu.SemaphoreType.DMA
    return pl.pallas_call(
        functools.partial(mixer, count, per_chunk),
        out_shape=pltpu.VMEM((tokens, width), jnp.bfloat16),
        in_specs=[hbm] * 7,
        out_specs=pl.BlockSpec(memory_space=pltpu.VMEM),
        scratch_shapes=[
            pltpu.VMEM((parts,) + conv_weight.shape[:1] + (width,), jnp.bfloat16),
            pltpu.VMEM(history.shape, jnp.bfloat16),
            pltpu.VMEM((poles, width), F32),
            pltpu.VMEM((poles, width), F32),
            pltpu.VMEM((1, width), F32),
            pltpu.VMEM((poles, width), F32),
            pltpu.VMEM((parts, 16, width), jnp.bfloat16),
            pltpu.VMEM((parts, tokens, width), jnp.bfloat16),
            pltpu.VMEM((parts, columns, tokens + 8, LANES), F32),
            pltpu.VMEM((columns, 8 * parts, LANES), F32),
            pltpu.VMEM((columns, length, SEG, LANES), F32),
            pltpu.VMEM((columns, length, SEG, LANES), F32),
            pltpu.VMEM((columns, length, SEG, LANES), F32),
            small, small, small, small, small, small, small,
            pltpu.VMEM((columns, length, LANES), F32),
            pltpu.VMEM((columns, poles, SEG, LANES), F32),
            pltpu.VMEM((columns, poles * SEG, LANES), F32),
            pltpu.VMEM((chunks, per_chunk, poles, LANES), F32),
            pltpu.VMEM((chunks, per_chunk, poles, LANES), F32),
            pltpu.VMEM((16, width), jnp.bfloat16),
            pltpu.VMEM((16, width), jnp.bfloat16),
            pltpu.VMEM((16, width // 2), jnp.bfloat16),
            pltpu.VMEM((16, width // 2), jnp.bfloat16),
            dma((chunks,)), dma((7,)), dma((chunks,)), dma((chunks,)),
            dma((2,)), dma((2,)),
        ],
        compiler_params=pltpu.CompilerParams(
            collective_id=0, has_side_effects=True, vmem_limit_bytes=60 * 1024 * 1024
        ),
    )(
        features.transpose(1, 0, 2), conv_weight.transpose(1, 0, 2), history,
        pole_rate, residue, skip_gain[None], start_state,
    )


def solution(mesh):
    return jax.shard_map(
        body,
        mesh=mesh,
        in_specs=(
            P(("grp", "seq"), None, "chan"),
            P(None, None, "chan"),
            P("grp", None, "chan"),
            P(None, "chan"),
            P(None, "chan"),
            P("chan"),
            P("grp", "chan"),
        ),
        out_specs=P(("grp", "seq"), "chan"),
        check_vma=False,
    )
```

```python
import functools

import jax
import jax.numpy as jnp
from jax import lax
from jax.experimental import pallas as pl
from jax.experimental.pallas import tpu as pltpu
from jax.sharding import PartitionSpec as P

MESH = pl.DeviceIdType.MESH
SEG = 8
LANES = 128
F32 = jnp.float32


def spread(row):
    return jnp.broadcast_to(row, (SEG, LANES))


def mixer(
    count, per_chunk,
    features, taps_in, history_in, rate_in, residue_in, skip_in, start_in,
    out,
    taps, history, rate, residue, skip, start, ends_here, held, ext, weight, prod, query, inner, decay, rest, seg1, seg2, seg4, whole,
    gain, filt, lift, scanned, send, recv, kv_send, kv_recv, q_send, q_recv,
    in_sem, own_sem, state_send, state_recv, halo_send, halo_recv,
):
    parts, tokens, width = held.shape
    margin = taps.shape[1] - 1
    length = tokens // SEG
    columns = width // LANES
    chunks = columns // per_chunk
    span = per_chunk * LANES
    half = width // 2
    poles = rate.shape[0]
    here = lax.axis_index("seq")
    first, last = here == 0, here == count - 1
    onward = lax.rem(here + 1, count)
    back = lax.rem(here + count - 1, count)

    def lanes(c):
        return pl.ds(pl.multiple_of(c * LANES, LANES), LANES)

    def fetch(k):
        area = pl.ds(pl.multiple_of(k * span, span), span)
        return pltpu.make_async_copy(features.at[:, :, area], held.at[:, :, area], in_sem.at[k])

    def state_copy(k):
        return pltpu.make_async_remote_copy(
            src_ref=send.at[k], dst_ref=recv.at[k], send_sem=state_send.at[k],
            recv_sem=state_recv.at[k], device_id={"seq": onward}, device_id_type=MESH,
        )

    def halo_copy(src, dst, k):
        return pltpu.make_async_remote_copy(
            src_ref=src, dst_ref=dst, send_sem=halo_send.at[k],
            recv_sem=halo_recv.at[k], device_id={"seq": onward}, device_id_type=MESH,
        )

    kv_copy = halo_copy(kv_send, kv_recv, 0)
    q_copy = halo_copy(q_send, q_recv, 1)

    barrier = pltpu.get_barrier_semaphore()

    @pl.when(jnp.logical_not(first))
    def _():
        pl.semaphore_signal(barrier, inc=1, device_id={"seq": back}, device_id_type=MESH)

    @pl.when(jnp.logical_not(last))
    def _():
        pl.semaphore_signal(barrier, inc=1, device_id={"seq": onward}, device_id_type=MESH)

    tail = pl.ds(tokens - 16, 16)
    owned = [
        pltpu.make_async_copy(src, dst, own_sem.at[i])
        for i, (src, dst) in enumerate(
            (
                (features.at[:, tail], ends_here),
                (rate_in, rate),
                (residue_in, residue),
                (skip_in, skip),
                (taps_in, taps),
                (start_in, start),
                (history_in, history),
            )
        )
    ]
    for copy in owned:
        copy.start()
    for k in range(chunks):
        fetch(k).start()

    rows = lax.broadcasted_iota(jnp.int32, (SEG, LANES), 0)

    def powers(one, two, four):
        value = jnp.where(rows % 2 == 1, one, 1.0)
        value = value * jnp.where((rows // 2) % 2 == 1, two, 1.0)
        return value * jnp.where(rows // 4 == 1, four, 1.0)

    def prepare(c, carry):
        r = rate[:, lanes(c)]
        decay[c] = jnp.exp(-r)
        rest[c] = jnp.exp(-float(length - margin) * r)
        seg1[c] = jnp.exp(-float(length) * r)
        seg2[c] = jnp.exp(-float(2 * length) * r)
        seg4[c] = jnp.exp(-float(4 * length) * r)
        whole[c] = jnp.exp(-float(tokens) * r)
        for j in range(parts):
            weight[c, j * 8 : j * 8 + margin + 1] = taps[j, :, lanes(c)].astype(F32)
        return carry

    def prepare_more(c, carry):
        r = rate[:, lanes(c)]
        g = residue[:, lanes(c)] * jnp.sqrt(2.0 * r) / 4.0
        a1 = decay[c]
        a2 = jnp.exp(-2.0 * r)
        a4 = jnp.exp(-4.0 * r)
        a8 = jnp.exp(-8.0 * r)
        s1, s2, s4 = seg1[c], seg2[c], seg4[c]
        gain[c] = g
        block = [jnp.zeros((SEG, LANES), F32) for _ in range(length // SEG)]
        for n in range(poles):
            part = spread(g[n : n + 1]) * powers(
                spread(a1[n : n + 1]), spread(a2[n : n + 1]), spread(a4[n : n + 1])
            )
            up = spread(a8[n : n + 1])
            for b in range(length // SEG):
                block[b] = block[b] + part
                part = part * up
            lift[c, n] = powers(
                spread(s1[n : n + 1]), spread(s2[n : n + 1]), spread(s4[n : n + 1])
            )
        direct = jnp.where(rows == 0, spread(skip[:, lanes(c)]), 0.0)
        block[0] = block[0] + direct
        for b in range(length // SEG):
            filt[c, b * SEG : (b + 1) * SEG] = block[b]
        return carry

    owned[0].wait()

    def pack(c, carry):
        k_rows = ends_here[1, :, lanes(c)].astype(F32)[8:]
        v_rows = ends_here[2, :, lanes(c)].astype(F32)[8:]
        kv_send[:, lanes(c)] = jnp.concatenate([k_rows, v_rows], axis=0).astype(jnp.bfloat16)
        return carry

    lax.fori_loop(0, columns, pack, 0)

    def pack_q(c, carry):
        low = ends_here[0, :, lanes(c)].astype(F32)[8:]
        high = ends_here[0, :, lanes(c + columns // 2)].astype(F32)[8:]
        q_send[:, lanes(c)] = jnp.concatenate([low, high], axis=0).astype(jnp.bfloat16)
        return carry

    lax.fori_loop(0, columns // 2, pack_q, 0)

    def greet():
        peers = jnp.where(first, 0, 1) + jnp.where(last, 0, 1)
        pl.semaphore_wait(barrier, peers)

        @pl.when(jnp.logical_not(last))
        def _():
            kv_copy.start()
            q_copy.start()

    def filtered(j, c, low, high):
        x = [ext[j, c, pl.ds(8 + i, SEG, stride=length), :] for i in range(low - margin, high)]
        w = [spread(weight[c, j * 8 + i : j * 8 + i + 1]) for i in range(margin + 1)]
        gained = []
        for t in range(high - low):
            value = w[0] * x[t + margin]
            for i in range(1, margin + 1):
                value = value + w[i] * x[t + margin - i]
            gained.append(value)
        return gained

    def product(c, low, high):
        p = [u * v for u, v in zip(filtered(1, c, low, high), filtered(2, c, low, high))]
        for t in range(low, high):
            prod[c, t] = p[t - low]
        return p

    def summed(c, n, p):
        a = spread(decay[c, n : n + 1])
        state = p[0]
        for value in p[1:]:
            state = a * state + value
        return state

    def shifted(value, by):
        return pltpu.roll(value, by, 0)

    def scan_segments(c, n, state):
        for by, ref in ((1, seg1), (2, seg2), (4, seg4)):
            step = jnp.where(rows >= by, spread(ref[c, n : n + 1]), 0.0)
            state = state + step * shifted(state, by)
        scanned[c, n * SEG : (n + 1) * SEG] = state

    def end_states(c, carry):
        p = product(c, 0, length)
        for n in range(poles):
            scan_segments(c, n, summed(c, n, p))
        return carry

    def end_states_early(c, carry):
        p = product(c, margin, length)
        for n in range(poles):
            scanned[c, n * SEG : (n + 1) * SEG] = summed(c, n, p)
        return carry

    def end_states_late(c, carry):
        p = product(c, 0, margin)
        for n in range(poles):
            early = scanned[c, n * SEG : (n + 1) * SEG]
            scan_segments(c, n, early + spread(rest[c, n : n + 1]) * summed(c, n, p))
        return carry

    def hand_on(k):
        for m in range(per_chunk):
            c = k * per_chunk + m
            ends = jnp.concatenate(
                [
                    scanned[c, pl.ds(b * 64 + SEG - 1, 8, stride=SEG), :]
                    for b in range(poles // 8)
                ],
                axis=0,
            )
            send[k, m] = whole[c] * recv[k, m] + ends
        state_copy(k).start()

    for copy in owned[1:]:
        copy.wait()
    lax.fori_loop(0, columns, prepare, 0)

    def widen(c, carry):
        for j in range(parts):
            ext[j, c, 8 : 8 + tokens] = held[j, :, lanes(c)].astype(F32)
        return carry

    def each(k, step):
        lax.fori_loop(k * per_chunk, (k + 1) * per_chunk, step, 0)

    @pl.when(first)
    def _():
        def begin(c, carry):
            recv[c // per_chunk, c % per_chunk] = start[:, lanes(c)]
            for i in range(margin):
                row = history[i, :, lanes(c)].astype(F32)
                for j in range(parts):
                    ext[j, c, 8 - margin + i : 9 - margin + i] = row[j : j + 1]
            return carry

        lax.fori_loop(0, columns, begin, 0)

        def only_pass(k, carry):
            fetch(k).wait()
            each(k, widen)
            each(k, end_states)

            @pl.when(k == 0)
            def _():
                greet()

            @pl.when(jnp.logical_not(last))
            def _():
                hand_on(k)

            return carry

        lax.fori_loop(0, chunks, only_pass, 0)

    @pl.when(jnp.logical_not(first))
    def _():
        greet()

        def early_pass(k, carry):
            fetch(k).wait()
            each(k, widen)
            each(k, end_states_early)
            return carry

        lax.fori_loop(0, chunks, early_pass, 0)
        kv_copy.wait_recv()
        q_copy.wait_recv()

        def unpack(c, carry):
            both = kv_recv[:, lanes(c)].astype(F32)
            ext[1, c, 0:8] = both[:8]
            ext[2, c, 0:8] = both[8:]
            return carry

        lax.fori_loop(0, columns, unpack, 0)

        def unpack_q(c, carry):
            both = q_recv[:, lanes(c)].astype(F32)
            ext[0, c, 0:8] = both[:8]
            ext[0, c + columns // 2, 0:8] = both[8:]
            return carry

        lax.fori_loop(0, columns // 2, unpack_q, 0)

        def late_pass(k, carry):
            each(k, end_states_late)

            @pl.when(jnp.logical_and(here == 1, jnp.logical_not(last)))
            def _():
                state_copy(k).wait_recv()
                hand_on(k)

            return carry

        lax.fori_loop(0, chunks, late_pass, 0)

    def inside(c, carry):
        q = filtered(0, c, 0, length)
        for t in range(length):
            query[c, t] = q[t]
        p = [prod[c, t] for t in range(length)]
        h = [spread(filt[c, i : i + 1]) for i in range(length)]
        for t in range(length):
            value = h[0] * p[t]
            for i in range(1, t + 1):
                value = value + h[i] * p[t - i]
            inner[c, t] = value
        return carry

    def second_pass(k, carry):
        @pl.when(jnp.logical_and(here > 1, jnp.logical_not(last)))
        def _():
            state_copy(k).wait_recv()
            hand_on(k)

        each(k, prepare_more)
        each(k, inside)
        return carry

    lax.fori_loop(0, chunks, second_pass, 0)

    def correct(c, carry):
        k, m = c // per_chunk, c % per_chunk
        w, a = [], []
        for n in range(poles):
            local = jnp.where(rows >= 1, shifted(scanned[c, n * SEG : (n + 1) * SEG], 1), 0.0)
            state = local + lift[c, n] * spread(recv[k, m, n : n + 1])
            w.append(spread(gain[c, n : n + 1]) * state)
            a.append(spread(decay[c, n : n + 1]))
        for t in range(length):
            w = [u * v for u, v in zip(w, a)]
            terms = list(w)
            while len(terms) > 1:
                terms = [terms[i] + terms[i + 1] for i in range(0, len(terms), 2)]
            value = query[c, t] * (inner[c, t] + terms[0])
            ext[0, c, pl.ds(t, SEG, stride=length), :] = value
        out[:, lanes(c)] = ext[0, c, 0:tokens].astype(jnp.bfloat16)
        return carry

    def third_pass(k, carry):
        @pl.when(jnp.logical_and(last, jnp.logical_not(first)))
        def _():
            state_copy(k).wait_recv()

        each(k, correct)
        return carry

    lax.fori_loop(0, chunks, third_pass, 0)

    @pl.when(jnp.logical_not(last))
    def _():
        kv_copy.wait_send()
        q_copy.wait_send()
        for k in range(chunks):
            state_copy(k).wait_send()


def body(features, conv_weight, history, pole_rate, residue, skip_gain, start_state):
    tokens, parts, width = features.shape
    poles = pole_rate.shape[0]
    columns = width // LANES
    per_chunk = 2
    chunks = columns // per_chunk
    length = tokens // SEG
    count = lax.axis_size("seq")
    hbm = pl.BlockSpec(memory_space=pltpu.HBM)
    small = pltpu.VMEM((columns, poles, LANES), F32)
    dma = pltpu.SemaphoreType.DMA
    return pl.pallas_call(
        functools.partial(mixer, count, per_chunk),
        out_shape=pltpu.VMEM((tokens, width), jnp.bfloat16),
        in_specs=[hbm] * 7,
        out_specs=pl.BlockSpec(memory_space=pltpu.VMEM),
        scratch_shapes=[
            pltpu.VMEM((parts,) + conv_weight.shape[:1] + (width,), jnp.bfloat16),
            pltpu.VMEM(history.shape, jnp.bfloat16),
            pltpu.VMEM((poles, width), F32),
            pltpu.VMEM((poles, width), F32),
            pltpu.VMEM((1, width), F32),
            pltpu.VMEM((poles, width), F32),
            pltpu.VMEM((parts, 16, width), jnp.bfloat16),
            pltpu.VMEM((parts, tokens, width), jnp.bfloat16),
            pltpu.VMEM((parts, columns, tokens + 8, LANES), F32),
            pltpu.VMEM((columns, 8 * parts, LANES), F32),
            pltpu.VMEM((columns, length, SEG, LANES), F32),
            pltpu.VMEM((columns, length, SEG, LANES), F32),
            pltpu.VMEM((columns, length, SEG, LANES), F32),
            small, small, small, small, small, small, small,
            pltpu.VMEM((columns, length, LANES), F32),
            pltpu.VMEM((columns, poles, SEG, LANES), F32),
            pltpu.VMEM((columns, poles * SEG, LANES), F32),
            pltpu.VMEM((chunks, per_chunk, poles, LANES), F32),
            pltpu.VMEM((chunks, per_chunk, poles, LANES), F32),
            pltpu.VMEM((16, width), jnp.bfloat16),
            pltpu.VMEM((16, width), jnp.bfloat16),
            pltpu.VMEM((16, width // 2), jnp.bfloat16),
            pltpu.VMEM((16, width // 2), jnp.bfloat16),
            dma((chunks,)), dma((7,)), dma((chunks,)), dma((chunks,)),
            dma((2,)), dma((2,)),
        ],
        compiler_params=pltpu.CompilerParams(
            collective_id=0, has_side_effects=True, vmem_limit_bytes=60 * 1024 * 1024
        ),
    )(
        features.transpose(1, 0, 2), conv_weight.transpose(1, 0, 2), history,
        pole_rate, residue, skip_gain[None], start_state,
    )


def solution(mesh):
    return jax.shard_map(
        body,
        mesh=mesh,
        in_specs=(
            P(("grp", "seq"), None, "chan"),
            P(None, None, "chan"),
            P("grp", None, "chan"),
            P(None, "chan"),
            P(None, "chan"),
            P("chan"),
            P("grp", "chan"),
        ),
        out_specs=P(("grp", "seq"), "chan"),
        check_vma=False,
    )
```

```python
import functools

import jax
import jax.numpy as jnp
from jax import lax
from jax.experimental import pallas as pl
from jax.experimental.pallas import tpu as pltpu
from jax.sharding import PartitionSpec as P

MESH = pl.DeviceIdType.MESH
SEG = 8
LANES = 128
F32 = jnp.float32


def spread(row):
    return jnp.broadcast_to(row, (SEG, LANES))


def mixer(
    count, per_chunk,
    features, taps_in, history_in, rate_in, residue_in, skip_in, start_in,
    out,
    taps, history, rate, residue, skip, start, ends_here, held, ext, weight, prod, query, inner, decay, rest, seg1, seg2, seg4, whole,
    gain, filt, lift, scanned, send, recv, kv_send, kv_recv, q_send, q_recv,
    in_sem, own_sem, state_send, state_recv, halo_send, halo_recv,
):
    parts, tokens, width = held.shape
    margin = taps.shape[1] - 1
    length = tokens // SEG
    columns = width // LANES
    chunks = columns // per_chunk
    span = per_chunk * LANES
    half = width // 2
    poles = rate.shape[0]
    here = lax.axis_index("seq")
    first, last = here == 0, here == count - 1
    onward = lax.rem(here + 1, count)
    back = lax.rem(here + count - 1, count)

    def lanes(c):
        return pl.ds(pl.multiple_of(c * LANES, LANES), LANES)

    def fetch(k):
        area = pl.ds(pl.multiple_of(k * span, span), span)
        return pltpu.make_async_copy(features.at[:, :, area], held.at[:, :, area], in_sem.at[k])

    def state_copy(k):
        return pltpu.make_async_remote_copy(
            src_ref=send.at[k], dst_ref=recv.at[k], send_sem=state_send.at[k],
            recv_sem=state_recv.at[k], device_id={"seq": onward}, device_id_type=MESH,
        )

    def halo_copy(src, dst, k):
        return pltpu.make_async_remote_copy(
            src_ref=src, dst_ref=dst, send_sem=halo_send.at[k],
            recv_sem=halo_recv.at[k], device_id={"seq": onward}, device_id_type=MESH,
        )

    kv_copy = halo_copy(kv_send, kv_recv, 0)
    q_copy = halo_copy(q_send, q_recv, 1)

    barrier = pltpu.get_barrier_semaphore()

    @pl.when(jnp.logical_not(first))
    def _():
        pl.semaphore_signal(barrier, inc=1, device_id={"seq": back}, device_id_type=MESH)

    @pl.when(jnp.logical_not(last))
    def _():
        pl.semaphore_signal(barrier, inc=1, device_id={"seq": onward}, device_id_type=MESH)

    tail = pl.ds(tokens - 16, 16)
    owned = [
        pltpu.make_async_copy(src, dst, own_sem.at[i])
        for i, (src, dst) in enumerate(
            (
                (features.at[:, tail], ends_here),
                (rate_in, rate),
                (residue_in, residue),
                (skip_in, skip),
                (taps_in, taps),
                (start_in, start),
                (history_in, history),
            )
        )
    ]
    for copy in owned:
        copy.start()
    for k in range(chunks):
        fetch(k).start()

    rows = lax.broadcasted_iota(jnp.int32, (SEG, LANES), 0)

    def powers(one, two, four):
        value = jnp.where(rows % 2 == 1, one, 1.0)
        value = value * jnp.where((rows // 2) % 2 == 1, two, 1.0)
        return value * jnp.where(rows // 4 == 1, four, 1.0)

    def prepare(c, carry):
        r = rate[:, lanes(c)]
        decay[c] = jnp.exp(-r)
        rest[c] = jnp.exp(-float(length - margin) * r)
        seg1[c] = jnp.exp(-float(length) * r)
        seg2[c] = jnp.exp(-float(2 * length) * r)
        seg4[c] = jnp.exp(-float(4 * length) * r)
        whole[c] = jnp.exp(-float(tokens) * r)
        for j in range(parts):
            weight[c, j * 8 : j * 8 + margin + 1] = taps[j, :, lanes(c)].astype(F32)
        return carry

    def prepare_more(c, carry):
        r = rate[:, lanes(c)]
        g = residue[:, lanes(c)] * jnp.sqrt(2.0 * r) / 4.0
        a1 = decay[c]
        a2 = jnp.exp(-2.0 * r)
        a4 = jnp.exp(-4.0 * r)
        a8 = jnp.exp(-8.0 * r)
        s1, s2, s4 = seg1[c], seg2[c], seg4[c]
        gain[c] = g
        block = [jnp.zeros((SEG, LANES), F32) for _ in range(length // SEG)]
        for n in range(poles):
            part = spread(g[n : n + 1]) * powers(
                spread(a1[n : n + 1]), spread(a2[n : n + 1]), spread(a4[n : n + 1])
            )
            up = spread(a8[n : n + 1])
            for b in range(length // SEG):
                block[b] = block[b] + part
                part = part * up
            lift[c, n] = powers(
                spread(s1[n : n + 1]), spread(s2[n : n + 1]), spread(s4[n : n + 1])
            )
        direct = jnp.where(rows == 0, spread(skip[:, lanes(c)]), 0.0)
        block[0] = block[0] + direct
        for b in range(length // SEG):
            filt[c, b * SEG : (b + 1) * SEG] = block[b]
        return carry

    owned[0].wait()

    def pack(c, carry):
        k_rows = ends_here[1, :, lanes(c)].astype(F32)[8:]
        v_rows = ends_here[2, :, lanes(c)].astype(F32)[8:]
        kv_send[:, lanes(c)] = jnp.concatenate([k_rows, v_rows], axis=0).astype(jnp.bfloat16)
        return carry

    lax.fori_loop(0, columns, pack, 0)

    def pack_q(c, carry):
        low = ends_here[0, :, lanes(c)].astype(F32)[8:]
        high = ends_here[0, :, lanes(c + columns // 2)].astype(F32)[8:]
        q_send[:, lanes(c)] = jnp.concatenate([low, high], axis=0).astype(jnp.bfloat16)
        return carry

    lax.fori_loop(0, columns // 2, pack_q, 0)

    peers = jnp.where(first, 0, 1) + jnp.where(last, 0, 1)
    pl.semaphore_wait(barrier, peers)

    @pl.when(jnp.logical_not(last))
    def _():
        kv_copy.start()
        q_copy.start()

    def filtered(j, c, low, high):
        x = [ext[j, c, pl.ds(8 + i, SEG, stride=length), :] for i in range(low - margin, high)]
        w = [spread(weight[c, j * 8 + i : j * 8 + i + 1]) for i in range(margin + 1)]
        gained = []
        for t in range(high - low):
            value = w[0] * x[t + margin]
            for i in range(1, margin + 1):
                value = value + w[i] * x[t + margin - i]
            gained.append(value)
        return gained

    def product(c, low, high):
        p = [u * v for u, v in zip(filtered(1, c, low, high), filtered(2, c, low, high))]
        for t in range(low, high):
            prod[c, t] = p[t - low]
        return p

    def summed(c, n, p):
        a = spread(decay[c, n : n + 1])
        state = p[0]
        for value in p[1:]:
            state = a * state + value
        return state

    def shifted(value, by):
        return pltpu.roll(value, by, 0)

    def scan_segments(c, n, state):
        for by, ref in ((1, seg1), (2, seg2), (4, seg4)):
            step = jnp.where(rows >= by, spread(ref[c, n : n + 1]), 0.0)
            state = state + step * shifted(state, by)
        scanned[c, n * SEG : (n + 1) * SEG] = state

    def end_states(c, carry):
        p = product(c, 0, length)
        for n in range(poles):
            scan_segments(c, n, summed(c, n, p))
        return carry

    def end_states_early(c, carry):
        p = product(c, margin, length)
        for n in range(poles):
            scanned[c, n * SEG : (n + 1) * SEG] = summed(c, n, p)
        return carry

    def end_states_late(c, carry):
        p = product(c, 0, margin)
        for n in range(poles):
            early = scanned[c, n * SEG : (n + 1) * SEG]
            scan_segments(c, n, early + spread(rest[c, n : n + 1]) * summed(c, n, p))
        return carry

    def hand_on(k):
        for m in range(per_chunk):
            c = k * per_chunk + m
            ends = jnp.concatenate(
                [
                    scanned[c, pl.ds(b * 64 + SEG - 1, 8, stride=SEG), :]
                    for b in range(poles // 8)
                ],
                axis=0,
            )
            send[k, m] = whole[c] * recv[k, m] + ends
        state_copy(k).start()

    for copy in owned[1:]:
        copy.wait()
    lax.fori_loop(0, columns, prepare, 0)

    def widen(c, carry):
        for j in range(parts):
            ext[j, c, 8 : 8 + tokens] = held[j, :, lanes(c)].astype(F32)
        return carry

    def each(k, step):
        lax.fori_loop(k * per_chunk, (k + 1) * per_chunk, step, 0)

    @pl.when(first)
    def _():
        def begin(c, carry):
            recv[c // per_chunk, c % per_chunk] = start[:, lanes(c)]
            for i in range(margin):
                row = history[i, :, lanes(c)].astype(F32)
                for j in range(parts):
                    ext[j, c, 8 - margin + i : 9 - margin + i] = row[j : j + 1]
            return carry

        lax.fori_loop(0, columns, begin, 0)

        def only_pass(k, carry):
            fetch(k).wait()
            each(k, widen)
            each(k, end_states)

            @pl.when(jnp.logical_not(last))
            def _():
                hand_on(k)

            return carry

        lax.fori_loop(0, chunks, only_pass, 0)

    @pl.when(jnp.logical_not(first))
    def _():
        def early_pass(k, carry):
            fetch(k).wait()
            each(k, widen)
            each(k, end_states_early)
            return carry

        lax.fori_loop(0, chunks, early_pass, 0)
        kv_copy.wait_recv()
        q_copy.wait_recv()

        def unpack(c, carry):
            both = kv_recv[:, lanes(c)].astype(F32)
            ext[1, c, 0:8] = both[:8]
            ext[2, c, 0:8] = both[8:]
            return carry

        lax.fori_loop(0, columns, unpack, 0)

        def unpack_q(c, carry):
            both = q_recv[:, lanes(c)].astype(F32)
            ext[0, c, 0:8] = both[:8]
            ext[0, c + columns // 2, 0:8] = both[8:]
            return carry

        lax.fori_loop(0, columns // 2, unpack_q, 0)

        def late_pass(k, carry):
            each(k, end_states_late)

            @pl.when(jnp.logical_and(here == 1, jnp.logical_not(last)))
            def _():
                state_copy(k).wait_recv()
                hand_on(k)

            return carry

        lax.fori_loop(0, chunks, late_pass, 0)

    def inside(c, carry):
        q = filtered(0, c, 0, length)
        for t in range(length):
            query[c, t] = q[t]
        p = [prod[c, t] for t in range(length)]
        h = [spread(filt[c, i : i + 1]) for i in range(length)]
        for t in range(length):
            value = h[0] * p[t]
            for i in range(1, t + 1):
                value = value + h[i] * p[t - i]
            inner[c, t] = value
        return carry

    def second_pass(k, carry):
        @pl.when(jnp.logical_and(here > 1, jnp.logical_not(last)))
        def _():
            state_copy(k).wait_recv()
            hand_on(k)

        each(k, prepare_more)
        each(k, inside)
        return carry

    lax.fori_loop(0, chunks, second_pass, 0)

    def correct(c, carry):
        k, m = c // per_chunk, c % per_chunk
        w, a = [], []
        for n in range(poles):
            local = jnp.where(rows >= 1, shifted(scanned[c, n * SEG : (n + 1) * SEG], 1), 0.0)
            state = local + lift[c, n] * spread(recv[k, m, n : n + 1])
            w.append(spread(gain[c, n : n + 1]) * state)
            a.append(spread(decay[c, n : n + 1]))
        for t in range(length):
            w = [u * v for u, v in zip(w, a)]
            terms = list(w)
            while len(terms) > 1:
                terms = [terms[i] + terms[i + 1] for i in range(0, len(terms), 2)]
            value = query[c, t] * (inner[c, t] + terms[0])
            ext[0, c, pl.ds(t, SEG, stride=length), :] = value
        out[:, lanes(c)] = ext[0, c, 0:tokens].astype(jnp.bfloat16)
        return carry

    def third_pass(k, carry):
        @pl.when(jnp.logical_and(last, jnp.logical_not(first)))
        def _():
            state_copy(k).wait_recv()

        each(k, correct)
        return carry

    lax.fori_loop(0, chunks, third_pass, 0)

    @pl.when(jnp.logical_not(last))
    def _():
        kv_copy.wait_send()
        q_copy.wait_send()
        for k in range(chunks):
            state_copy(k).wait_send()


def body(features, conv_weight, history, pole_rate, residue, skip_gain, start_state):
    tokens, parts, width = features.shape
    poles = pole_rate.shape[0]
    columns = width // LANES
    per_chunk = 1
    chunks = columns // per_chunk
    length = tokens // SEG
    count = lax.axis_size("seq")
    hbm = pl.BlockSpec(memory_space=pltpu.HBM)
    small = pltpu.VMEM((columns, poles, LANES), F32)
    dma = pltpu.SemaphoreType.DMA
    return pl.pallas_call(
        functools.partial(mixer, count, per_chunk),
        out_shape=pltpu.VMEM((tokens, width), jnp.bfloat16),
        in_specs=[hbm] * 7,
        out_specs=pl.BlockSpec(memory_space=pltpu.VMEM),
        scratch_shapes=[
            pltpu.VMEM((parts,) + conv_weight.shape[:1] + (width,), jnp.bfloat16),
            pltpu.VMEM(history.shape, jnp.bfloat16),
            pltpu.VMEM((poles, width), F32),
            pltpu.VMEM((poles, width), F32),
            pltpu.VMEM((1, width), F32),
            pltpu.VMEM((poles, width), F32),
            pltpu.VMEM((parts, 16, width), jnp.bfloat16),
            pltpu.VMEM((parts, tokens, width), jnp.bfloat16),
            pltpu.VMEM((parts, columns, tokens + 8, LANES), F32),
            pltpu.VMEM((columns, 8 * parts, LANES), F32),
            pltpu.VMEM((columns, length, SEG, LANES), F32),
            pltpu.VMEM((columns, length, SEG, LANES), F32),
            pltpu.VMEM((columns, length, SEG, LANES), F32),
            small, small, small, small, small, small, small,
            pltpu.VMEM((columns, length, LANES), F32),
            pltpu.VMEM((columns, poles, SEG, LANES), F32),
            pltpu.VMEM((columns, poles * SEG, LANES), F32),
            pltpu.VMEM((chunks, per_chunk, poles, LANES), F32),
            pltpu.VMEM((chunks, per_chunk, poles, LANES), F32),
            pltpu.VMEM((16, width), jnp.bfloat16),
            pltpu.VMEM((16, width), jnp.bfloat16),
            pltpu.VMEM((16, width // 2), jnp.bfloat16),
            pltpu.VMEM((16, width // 2), jnp.bfloat16),
            dma((chunks,)), dma((7,)), dma((chunks,)), dma((chunks,)),
            dma((2,)), dma((2,)),
        ],
        compiler_params=pltpu.CompilerParams(
            collective_id=0, has_side_effects=True, vmem_limit_bytes=60 * 1024 * 1024
        ),
    )(
        features.transpose(1, 0, 2), conv_weight.transpose(1, 0, 2), history,
        pole_rate, residue, skip_gain[None], start_state,
    )


def solution(mesh):
    return jax.shard_map(
        body,
        mesh=mesh,
        in_specs=(
            P(("grp", "seq"), None, "chan"),
            P(None, None, "chan"),
            P("grp", None, "chan"),
            P(None, "chan"),
            P(None, "chan"),
            P("chan"),
            P("grp", "chan"),
        ),
        out_specs=P(("grp", "seq"), "chan"),
        check_vma=False,
    )
```
